256 devices in a mesh: grp: 16 (over y, x), mem: 16 (over z, core).
Axes of the slice: x: 4, y: 4, z: 8, core: 2. Of those that a mesh axis runs over, the one named last changes fastest.
Arguments:
- embedding: bfloat16 [262144, 768], P(('grp', 'mem')), parts along dimension 0, may hold values from -127 to 127, as said below
- row_scale: float32 [262144], P(('grp', 'mem')), parts along dimension 0, may hold values from 0.0004 to 0.0006
- block_rows: int32 [512], P(('grp', 'mem')), parts along dimension 0, may hold values from 1 to 512, 12288 in all
- requests: int32 [256, 16], P(('grp', 'mem')), parts along dimension 0, may hold values from 0 to 1
Outputs:
- highest: float32 [262144], P(('grp', 'mem')), parts along dimension 0
The draws below stay inside these ranges and needn't reach their ends.
There are 16 independent parts, one for each index of `grp`. The reference program is written for one: setup_inputs(seed, part) draws one part's arguments, and reference() takes and returns one part's arrays. A program takes and returns all parts, laid end to end along the dimension named above; each array names one. Nothing has to cross between parts.
Inputs may be any that keep to these rules, and one draw needn't show every extreme that they name: `embedding`: whole numbers, held exactly. `block_rows`: the largest block holds exactly 512 live rows.
All inputs are finite; a program needn't handle non-finite values.
Results may differ from the reference program's by a relative error of at most 0.0012.
Values may be sent and summed in bfloat16 or wider, within the bound.
No kernel may reach another device: no remote copies, remote signals or barrier semaphores. Data moves between devices by JAX's collectives and lax.ppermute only.
A program may use at most 128 MiB of HBM per device.

```python
import math
import jax
import jax.numpy as jnp
import numpy as np
from jax import lax

D = 768
BLOCK = 512
BLK_DEV = 2
NBLK = 32
ROWS = 16384
N_MEM = 16


def draw_embedding(key, part):
    key = jax.random.fold_in(key, 11)
    first = jax.random.fold_in(key, 0)
    codes = jax.random.randint(first, (ROWS, D), -127, 128, dtype=jnp.int32)
    return codes.astype(jnp.bfloat16)


def set_ends(values, stream_key, smallest, high):
    longest = values.shape.index(max(values.shape))
    spots = []
    for shift in (0, 1):
        where = [jax.random.randint(jax.random.fold_in(stream_key, axis), (), 0, length) for axis, length in enumerate(values.shape)]
        where[longest] = (where[longest] + shift) % values.shape[longest]
        spots.append(tuple(where))
    return values.at[spots[0]].set(smallest).at[spots[1]].set(high)


def block_levels(stream_key, shape, pieces, smallest, largest):
    gain, own = 1.0, jax.random.fold_in(stream_key, 6)
    for axis_at, blocks in pieces:
        heights = jnp.exp(jax.random.uniform(jax.random.fold_in(own, axis_at), (blocks,), jnp.float32, smallest / len(pieces), largest / len(pieces)))
        gain = gain * jnp.repeat(heights, shape[axis_at] // blocks).reshape([-1 if axis == axis_at else 1 for axis in range(len(shape))])
    return gain


def length_profile(amount, total, bound, lean):
    loads = [(1 << 20) // math.isqrt(standing ** lean) + 1 for standing in range(2, amount + 1)]
    spare, holding = total - bound - (amount - 1), [1] * (amount - 1)
    while spare > 0:
        free = [i for i in range(amount - 1) if holding[i] < bound]
        mass, budget = sum([loads[i] for i in free]), spare
        for i in free:
            extra = min(bound - holding[i], max(1, budget * loads[i] // mass), spare)
            holding[i] = holding[i] + extra
            spare = spare - extra
    return np.array([bound] + holding)


def ragged(stream_key, number_of, total, limit, skew):
    if number_of == 2:
        one = jax.random.randint(stream_key, (), max(1, total - limit), min(limit, total - 1) + 1)
        return jnp.stack([one, total - one])
    sizes = jnp.asarray(length_profile(number_of, total, limit, skew), jnp.int32)
    pairs = (number_of - 1) // 2
    source_of, sink = sizes[1:1 + 2 * pairs:2], sizes[2:2 + 2 * pairs:2]
    margin = jnp.minimum(source_of - 1, limit - sink)
    shifted = jax.random.randint(jax.random.fold_in(stream_key, 1), (pairs,), 0, 1 << 20) % (margin + 1)
    sizes = sizes.at[1:1 + 2 * pairs:2].set(source_of - shifted).at[2:2 + 2 * pairs:2].set(sink + shifted)
    return sizes[jax.random.permutation(jax.random.fold_in(stream_key, 2), number_of)]


def setup_inputs(seed: int = 0, part: int = 0) -> dict:
    arg_keys = jax.random.split(jax.random.key(seed), 5)
    own_keys = jax.random.split(jax.random.fold_in(arg_keys[4], part), 5)
    embedding = draw_embedding(jax.random.fold_in(jax.random.fold_in(arg_keys[4], part), 71), part)
    row_scale = jnp.clip(jnp.exp(math.log(0.0006) - 0.4054652 * jax.random.uniform(own_keys[1], (ROWS,), jnp.float32) ** block_levels(own_keys[1], (ROWS,), ((0, 16),), -0.2, 0.2)), 0.0004, 0.0006)
    block_rows = ragged(own_keys[2], NBLK, NBLK * BLOCK * 3 // 4, BLOCK, 2).astype(jnp.int32)
    requests = set_ends(jax.random.randint(own_keys[3], (N_MEM, N_MEM), 0, BLK_DEV), jax.random.fold_in(own_keys[3], 1), 0, BLK_DEV - 1).astype(jnp.int32)
    return dict(embedding=embedding, row_scale=row_scale, block_rows=block_rows, requests=requests)


def reference(embedding, row_scale, block_rows, requests):
    blocks_all = block_rows.shape[0]
    per_device = blocks_all // N_MEM
    decoded = (embedding.astype(jnp.float32) * row_scale[:, None]).astype(jnp.bfloat16)
    decoded = decoded.reshape(blocks_all, BLOCK, decoded.shape[1])
    positions = jnp.arange(BLOCK, dtype=jnp.int32)
    live = positions[None, :] < block_rows[:, None]
    asker = jnp.arange(N_MEM, dtype=jnp.int32)[:, None, None]
    owner = jnp.arange(N_MEM, dtype=jnp.int32)[None, :, None]
    local = jnp.arange(per_device, dtype=jnp.int32)[None, None, :]
    shape = (N_MEM, N_MEM, per_device)
    left_block = jnp.broadcast_to(asker * per_device + local, shape).reshape(-1).astype(jnp.int32)
    right_block = jnp.broadcast_to(owner * per_device + requests[:, :, None], shape).reshape(-1).astype(jnp.int32)
    identity = positions[:, None] == positions[None, :]

    def visit(running, entries):
        left, right = entries
        scores = jnp.dot(decoded[left], decoded[right].T, preferred_element_type=jnp.float32)
        allowed = live[right][None, :] & jnp.logical_not(identity & (left == right))
        masked = jnp.where(allowed, scores, jnp.float32(-1e30))
        running = running.at[left].max(jnp.max(masked, axis=1))
        column = jnp.max(jnp.where(live[left][:, None], masked, jnp.float32(-1e30)), axis=0)
        running = running.at[right].max(column)
        return running, None

    start = jnp.full((blocks_all, BLOCK), -1e30, dtype=jnp.float32)
    highest, _ = lax.scan(visit, start, (left_block, right_block))
    return jnp.where(live, highest, jnp.float32(0.0)).reshape(-1)
```

```python
import functools

import jax
import jax.numpy as jnp
from jax import lax
from jax.experimental import pallas as pl
from jax.experimental.pallas import tpu as pltpu
from jax.sharding import PartitionSpec as P

BLOCK = 512
META = 16
LOWEST = -1e30
CHIPS = 8
OWN, SIB, UP1, DOWN1, SIBDOWN1, UP2, DOWN2 = range(7)


def hop(step, flip_from=None):
    pairs = []
    for chip in range(CHIPS):
        target = (chip + step) % CHIPS
        for core in range(2):
            crossed = flip_from is not None and target >= flip_from
            pairs.append((chip * 2 + core, target * 2 + (1 - core if crossed else core)))
    return pairs


SIBLING = [(device, device ^ 1) for device in range(2 * CHIPS)]


def listens(meta, asked):
    row = meta[0:1, 0:128].astype(jnp.float32)
    lane = lax.broadcasted_iota(jnp.int32, (1, 128), 1)
    return jnp.max(jnp.where(lane == asked, row, 0.0))


def score_tile(x, y):
    return lax.dot_general(x, y, (((1,), (1,)), ((), ())), preferred_element_type=jnp.float32)


def pair_blocks(x_ref, y_ref, row_acc, col_acc):
    for n in range(0, BLOCK, 256):
        scores = score_tile(x_ref[0:BLOCK, :], y_ref[n : n + 256, :])
        row_acc[...] = jnp.maximum(row_acc[...], jnp.maximum(scores[:, 0:128], scores[:, 128:256]))
        col_acc[:, n : n + 256] = jnp.maximum(
            col_acc[:, n : n + 256], jnp.max(scores.reshape(BLOCK // 8, 8, 256), axis=0)
        )


def rows_to_lanes(row_acc):
    return jnp.max(row_acc[...].T, axis=0, keepdims=True)


def raise_row(best, item, block, values):
    span = slice(block * BLOCK, (block + 1) * BLOCK)
    best[item : item + 1, span] = jnp.maximum(best[item : item + 1, span], values)


def cross_kernel(plan, n_blocks, last, ids, *refs):
    data = refs[:n_blocks]
    best_in = refs[n_blocks]
    best_out = refs[n_blocks + 1]
    scratch = refs[n_blocks + 2 :]
    if last:
        best, scratch = scratch[0], scratch[1:]
    else:
        best = best_out
    best[...] = best_in[...]
    xs, ys = [], []
    for x, y in plan:
        if x not in xs:
            xs.append(x)
        if y not in ys:
            ys.append(y)
    row_accs = dict(zip(xs, scratch[: len(xs)]))
    col_accs = dict(zip(ys, scratch[len(xs) : len(xs) + len(ys)]))
    for acc in list(row_accs.values()) + list(col_accs.values()):
        acc[...] = jnp.full(acc.shape, LOWEST, jnp.float32)
    asks = {}
    for x, y in plan:
        key = (x[0], y[0])
        if key not in asks:
            asks[key] = (
                listens(data[x[3]][BLOCK : BLOCK + META, :], ids[y[0]]),
                listens(data[y[3]][BLOCK : BLOCK + META, :], ids[x[0]]),
            )
    for x, y in plan:
        x_asks, y_asks = asks[(x[0], y[0])]
        listed = (x_asks == float(y[1])) | (y_asks == float(x[1]))

        @pl.when(listed)
        def _():
            pair_blocks(data[x[2]], data[y[2]], row_accs[x], col_accs[y])

    for x in xs:
        raise_row(best, x[0], x[1], rows_to_lanes(row_accs[x]))
    for y in ys:
        raise_row(best, y[0], y[1], jnp.max(col_accs[y][...], axis=0, keepdims=True))
    if last:
        best_out[...] = jnp.full(best_out.shape, LOWEST, jnp.float32)
        for item in range(7):
            for part in range(8):
                best_out[ids[item], part : part + 1, :] = best[item : item + 1, part * 128 : (part + 1) * 128]


def cross_call(plan_items, arrays, best, ids, last=False):
    order = sorted({b for pair in plan_items for b in pair} | {(b[0], 0) for pair in plan_items for b in pair})
    number = {b: i for i, b in enumerate(order)}
    plan = [tuple((b[0], b[1], number[b], number[(b[0], 0)]) for b in pair) for pair in plan_items]
    n_x = len({x for x, _ in plan})
    n_y = len({y for _, y in plan})
    vmem = pl.BlockSpec(memory_space=pltpu.VMEM)
    scratch = [pltpu.VMEM((BLOCK, 128), jnp.float32)] * n_x + [pltpu.VMEM((8, BLOCK), jnp.float32)] * n_y
    if last:
        scratch = [pltpu.VMEM((8, 2 * BLOCK), jnp.float32)] + scratch
        out = jax.ShapeDtypeStruct((2 * CHIPS, 8, 128), jnp.float32)
    else:
        out = jax.ShapeDtypeStruct((8, 2 * BLOCK), jnp.float32)
    width = arrays[order[0]].shape[1]
    return pl.pallas_call(
        functools.partial(cross_kernel, plan, len(order), last),
        out_shape=out,
        in_specs=[pl.BlockSpec(memory_space=pltpu.SMEM)] + [vmem] * (len(order) + 1),
        out_specs=vmem,
        scratch_shapes=scratch,
        compiler_params=pltpu.CompilerParams(vmem_limit_bytes=28 * 1024 * 1024),
        cost_estimate=pl.CostEstimate(
            flops=2 * len(plan) * BLOCK * BLOCK * width, bytes_accessed=len(order) * BLOCK * width * 2, transcendentals=0
        ),
    )(ids, *[arrays[b] for b in order], best)


def own_kernel(ids, rows, own_a, own_b, sib_a, sib_b, best, row_acc, row_acc_b, col_a, col_b):
    best[...] = jnp.full(best.shape, LOWEST, jnp.float32)
    mine, theirs = ids[OWN], ids[SIB]
    core = lax.rem(mine, 2)
    my_meta = own_a[BLOCK : BLOCK + META, :]
    asks_self = listens(my_meta, mine)
    asks_sib = listens(my_meta, theirs)
    sib_asks = listens(sib_a[BLOCK : BLOCK + META, :], mine)
    for acc in (row_acc, row_acc_b, col_a, col_b):
        acc[...] = jnp.full(acc.shape, LOWEST, jnp.float32)

    for half, own in enumerate((own_a, own_b)):

        @pl.when(asks_self == float(half))
        def _():
            live = rows[half]
            for n in range(0, BLOCK, 256):
                scores = score_tile(own[0:BLOCK, :], own[n : n + 256, :])
                i = lax.broadcasted_iota(jnp.int32, scores.shape, 0)
                j = lax.broadcasted_iota(jnp.int32, scores.shape, 1) + n
                scores = jnp.where((i != j) & (i < live), scores, LOWEST)
                raise_row_part(best, OWN, half * BLOCK + n, jnp.max(scores, axis=0, keepdims=True))

    pair_blocks(own_a, own_b, row_acc, col_b)
    raise_row(best, OWN, 0, rows_to_lanes(row_acc))
    raise_row(best, OWN, 1, jnp.max(col_b[...], axis=0, keepdims=True))

    for acc in (row_acc, row_acc_b, col_a, col_b):
        acc[...] = jnp.full(acc.shape, LOWEST, jnp.float32)
    for half, own, acc in ((0, own_a, row_acc), (1, own_b, row_acc_b)):
        for other, sib, col in ((0, sib_a, col_a), (1, sib_b, col_b)):
            wanted = (asks_sib == float(other)) | (sib_asks == float(half))
            if other == 1:
                turn = core == 1
                if half == 0:
                    continue
            elif half == 0:
                turn = core == 0
            else:
                turn = True

            @pl.when(wanted & turn)
            def _():
                pair_blocks(own, sib, acc, col)

    raise_row(best, OWN, 0, rows_to_lanes(row_acc))
    raise_row(best, OWN, 1, rows_to_lanes(row_acc_b))
    raise_row(best, SIB, 0, jnp.max(col_a[...], axis=0, keepdims=True))
    raise_row(best, SIB, 1, jnp.max(col_b[...], axis=0, keepdims=True))


def raise_row_part(best, item, start, values):
    span = slice(start, start + values.shape[1])
    best[item : item + 1, span] = jnp.maximum(best[item : item + 1, span], values)


def own_call(ids, rows, own, sib):
    vmem = pl.BlockSpec(memory_space=pltpu.VMEM)
    smem = pl.BlockSpec(memory_space=pltpu.SMEM)
    row_acc = pltpu.VMEM((BLOCK, 128), jnp.float32)
    col_acc = pltpu.VMEM((8, BLOCK), jnp.float32)
    width = own[0].shape[1]
    return pl.pallas_call(
        own_kernel,
        out_shape=jax.ShapeDtypeStruct((8, 2 * BLOCK), jnp.float32),
        in_specs=[smem, smem] + [vmem] * 4,
        out_specs=vmem,
        scratch_shapes=[row_acc, row_acc, col_acc, col_acc],
        compiler_params=pltpu.CompilerParams(vmem_limit_bytes=28 * 1024 * 1024),
        cost_estimate=pl.CostEstimate(
            flops=2 * 5 * BLOCK * BLOCK * width, bytes_accessed=4 * BLOCK * width * 2, transcendentals=0
        ),
    )(ids, rows, *own, *sib)


def shards(embedding, row_scale, block_rows, requests):
    width = embedding.shape[1]
    myself = lax.axis_index("mem").astype(jnp.int32)
    chip, core = myself // 2, myself % 2
    positions = jnp.arange(BLOCK, dtype=jnp.int32)

    def decode(block):
        span = slice(block * BLOCK, (block + 1) * BLOCK)
        values = (embedding[span].astype(jnp.float32) * row_scale[span, None]).astype(jnp.bfloat16)
        return jnp.where((positions < block_rows[block])[:, None], values, values[0:1])

    meta = jnp.zeros((META, width), jnp.bfloat16).at[0, 0 : 2 * CHIPS].set(requests[0].astype(jnp.bfloat16))
    own = (jnp.concatenate([decode(0), meta], axis=0), decode(1))

    def at(step):
        return lax.rem(chip + step + CHIPS, CHIPS)

    up2_core = jnp.where(chip >= CHIPS // 2, 1 - core, core)
    ids = jnp.stack(
        [
            myself,
            chip * 2 + 1 - core,
            at(-1) * 2 + core,
            at(1) * 2 + core,
            at(1) * 2 + 1 - core,
            at(-2) * 2 + up2_core,
            at(2) * 2 + core,
            myself,
        ]
    ).astype(jnp.int32)

    def send(values, pairs):
        return lax.ppermute(values, "mem", pairs)

    up1 = [send(own[0], hop(1)), None]
    down1 = [send(own[0], hop(-1)), None]
    up1[1] = send(own[1], hop(1))
    down1[1] = send(own[1], hop(-1))
    sib = [send(part, SIBLING) for part in own]
    up2, down2, sibdown1 = [], [], []
    for half in range(2):
        up2.append(send(up1[half], hop(1, CHIPS // 2)))
        down2.append(send(down1[half], hop(-1)))
        sibdown1.append(send(down1[half], SIBLING))

    arrays = {}
    for item, parts in ((OWN, own), (SIB, sib), (UP1, up1), (DOWN1, down1), (SIBDOWN1, sibdown1), (UP2, up2), (DOWN2, down2)):
        for half in range(2):
            arrays[(item, half)] = parts[half]

    def all_pairs(left, right):
        return [((left, a), (right, b)) for a in range(2) for b in range(2)]

    best = own_call(ids, block_rows, own, sib)
    best = cross_call(all_pairs(OWN, DOWN1) + all_pairs(OWN, SIBDOWN1), arrays, best, ids)
    best = cross_call(all_pairs(UP1, DOWN1) + all_pairs(UP1, SIBDOWN1), arrays, best, ids)
    early = [((UP2, 0), (item, b)) for item in (DOWN1, SIBDOWN1) for b in range(2)] + [((UP2, 0), (DOWN2, 0))]
    best = cross_call(early, arrays, best, ids)
    late = [((UP2, 1), (item, b)) for item in (DOWN1, SIBDOWN1) for b in range(2)]
    late += [((UP2, 1), (DOWN2, 0)), ((UP2, 1), (DOWN2, 1)), ((UP2, 0), (DOWN2, 1))]
    partial = cross_call(late, arrays, best, ids, last=True)

    returned = lax.all_to_all(partial, "mem", split_axis=0, concat_axis=0, tiled=True)
    highest = jnp.max(returned, axis=0).reshape(2, BLOCK)
    live = positions[None, :] < block_rows[:, None]
    return jnp.where(live, highest, jnp.float32(0.0)).reshape(-1)


def solution(mesh):
    return jax.shard_map(
        shards,
        mesh=mesh,
        in_specs=(
            P(("grp", "mem"), None),
            P(("grp", "mem")),
            P(("grp", "mem")),
            P(("grp", "mem"), None),
        ),
        out_specs=P(("grp", "mem")),
        check_vma=False,
    )
```

```python
import functools

import jax
import jax.numpy as jnp
from jax import lax
from jax.experimental import pallas as pl
from jax.experimental.pallas import tpu as pltpu
from jax.sharding import PartitionSpec as P

BLOCK = 512
ROWS = 2 * BLOCK
META = 16
TILE = 256
LOWEST = -1e30
CHIPS = 8
PIECES = ((0, 768), (768, 256))
LAST = len(PIECES) - 1
OWN, SIB, BELOW1, ABOVE1, BELOW2, ABOVE2 = range(6)
ABOVE1_CROSSED = (1,) * CHIPS
ABOVE2_CROSSED = (0, 0, 0, 0, 1, 0, 1, 0)
BELOW2_CROSSED = tuple(ABOVE2_CROSSED[chip - 1] for chip in range(CHIPS))
ABOVE2_STRAIGHT = tuple(1 - crossed for crossed in ABOVE2_CROSSED)
BELOW2_STRAIGHT = tuple(ABOVE2_CROSSED[chip - 2] for chip in range(CHIPS))
VMEM = pl.BlockSpec(memory_space=pltpu.VMEM)
SMEM = pl.BlockSpec(memory_space=pltpu.SMEM)
ANY = pl.BlockSpec(memory_space=pl.ANY)
PARAMS = pltpu.CompilerParams(vmem_limit_bytes=20 * 1024 * 1024)


def hop(step, crossed=(0,) * CHIPS):
    pairs = []
    for chip in range(CHIPS):
        target = (chip + step) % CHIPS
        for core in range(2):
            pairs.append((chip * 2 + core, target * 2 + (core ^ crossed[target])))
    return pairs


SIBLING = [(device, device ^ 1) for device in range(2 * CHIPS)]


def in_vmem(values):
    return pltpu.with_memory_space_constraint(values, pltpu.VMEM)


def decode_kernel(pieces, rows_hbm, scale_hbm, requests_hbm, codes, *refs):
    outs = refs[: len(pieces)]
    rows, scale, requests, head, held, arrived = refs[len(pieces) :]
    start = PIECES[pieces[0]][0]
    count = sum(PIECES[p][1] for p in pieces)
    above = start - start % BLOCK
    small = [
        pltpu.make_async_copy(source, target, arrived.at[count // 128 + n])
        for n, (source, target) in enumerate(
            ((rows_hbm, rows), (scale_hbm, scale), (requests_hbm, requests), (codes.at[pl.ds(above, META), :], head))
        )
    ]
    copies = [
        pltpu.make_async_copy(codes.at[pl.ds(start + n, 128), :], held.at[pl.ds(n, 128), :], arrived.at[n // 128])
        for n in range(0, count, 128)
    ]
    for copy in small + copies:
        copy.start()
    for copy in small:
        copy.wait()
    width = codes.shape[1]
    first = {}
    factor = jnp.broadcast_to(scale[above // 128 : above // 128 + 1, :], (128, 128)).T
    for lane in range(0, width, 128):
        first[lane] = head[0:1, lane : lane + 128].astype(jnp.float32) * factor[0:1, :]
    for out, piece in zip(outs, pieces):
        for n in range(0, PIECES[piece][1], 128):
            at = PIECES[piece][0] + n
            block, into = at // BLOCK, at - start
            copies[into // 128].wait()
            factor = jnp.broadcast_to(scale[at // 128 : at // 128 + 1, :], (128, 128)).T
            live = lax.broadcasted_iota(jnp.int32, (128, 128), 0) + at % BLOCK < rows[block]
            for lane in range(0, width, 128):
                values = held[into : into + 128, lane : lane + 128].astype(jnp.float32) * factor
                if at % BLOCK == 0:
                    first[lane] = values[0:1, :]
                out[n : n + 128, lane : lane + 128] = jnp.where(live, values, first[lane]).astype(jnp.bfloat16)
    if pieces[0] == 0:
        count = PIECES[0][1]
        outs[0][count : count + META, :] = jnp.zeros((META, width), jnp.bfloat16)
        asked = jnp.broadcast_to(requests[...].astype(jnp.float32), (META, requests.shape[1]))
        outs[0][count : count + META, 0 : requests.shape[1]] = asked.astype(jnp.bfloat16)


def decode_call(pieces, rows, scale, requests, codes):
    width = codes.shape[1]
    count = sum(PIECES[p][1] for p in pieces)
    return pl.pallas_call(
        functools.partial(decode_kernel, pieces),
        out_shape=[pltpu.VMEM((PIECES[p][1] + (META if p == 0 else 0), width), jnp.bfloat16) for p in pieces],
        in_specs=[ANY] * 4,
        out_specs=[VMEM] * len(pieces),
        scratch_shapes=[
            pltpu.SMEM(rows.shape, rows.dtype),
            pltpu.VMEM(scale.shape, scale.dtype),
            pltpu.VMEM(requests.shape, requests.dtype),
            pltpu.VMEM((META, width), jnp.bfloat16),
            pltpu.VMEM((count, width), jnp.bfloat16),
            pltpu.SemaphoreType.DMA((count // 128 + 4,)),
        ],
        compiler_params=PARAMS,
    )(*[pltpu.with_memory_space_constraint(a, pltpu.HBM) for a in (rows, scale, requests, codes)])


def listens(meta, asked):
    row = meta[0:1, 0:128].astype(jnp.float32)
    lane = lax.broadcasted_iota(jnp.int32, (1, 128), 1)
    return jnp.max(jnp.where(lane == asked, row, 0.0))


def score_tile(x, y):
    return lax.dot_general(x, y, (((1,), (1,)), ((), ())), preferred_element_type=jnp.float32)


def segments(piece):
    start, count = PIECES[piece]
    cuts = sorted({start, start + count} | {c for c in range(0, ROWS, BLOCK) if start < c < start + count})
    return [(a - start, a, b - a) for a, b in zip(cuts, cuts[1:])]


def raise_row(best, item, start, values):
    span = slice(start, start + values.shape[1])
    best[item : item + 1, span] = jnp.maximum(best[item : item + 1, span], values)


def score_kernel(plan, order, kind, ids, *refs):
    data = dict(zip(order, refs))
    extra = refs[len(order)]
    out = refs[len(order) + 1]
    scratch = list(refs[len(order) + 2 :])
    best = scratch.pop(0) if kind == "last" else out
    best[...] = jnp.full(best.shape, LOWEST, jnp.float32) if kind == "first" else extra[...]
    row_accs, col_accs = {}, {}
    for x, y, _ in plan:
        row_accs.setdefault(x, None)
        col_accs.setdefault(y, None)
    for accs in (row_accs, col_accs):
        for piece in accs:
            accs[piece] = scratch.pop(0)
            accs[piece][...] = jnp.full(accs[piece].shape, LOWEST, jnp.float32)
    asks = {}
    count0 = PIECES[0][1]
    for x, y, _ in plan:
        for a, b in ((x[0], y[0]), (y[0], x[0])):
            if (a, b) not in asks:
                asks[(a, b)] = listens(data[(a, 0)][count0 : count0 + META, :], ids[b])
    core = lax.rem(ids[OWN], 2)
    straight = {ABOVE2: ids[6], BELOW2: ids[7]}

    def meet(x, x_at, x_row, x_rows, y, y_at, y_row, y_rows, listed, itself):
        scores = score_tile(data[x][x_at : x_at + x_rows, :], data[y][y_at : y_at + y_rows, :])
        if itself:
            i = lax.broadcasted_iota(jnp.int32, scores.shape, 0) + x_row % BLOCK
            j = lax.broadcasted_iota(jnp.int32, scores.shape, 1) + y_row % BLOCK
            live = extra[x_row // BLOCK]
            scores = jnp.where((i != j) & (i < live) & (j < live), scores, LOWEST)
        rows = functools.reduce(jnp.maximum, [scores[:, n : n + 128] for n in range(0, y_rows, 128)])
        cols = jnp.max(scores.reshape(x_rows // 8, 8, y_rows), axis=0)
        row_acc, col_acc = row_accs[x], col_accs[y]
        here, there = slice(x_at, x_at + x_rows), slice(y_at, y_at + y_rows)
        row_acc[here, :] = jnp.maximum(row_acc[here, :], jnp.where(listed, rows, LOWEST))
        col_acc[:, there] = jnp.maximum(col_acc[:, there], jnp.where(listed, cols, LOWEST))
    def visit(x, y, when):
        for x_at, x_row, x_rows in segments(x[1]):
            for y_at, y_row, y_rows in segments(y[1]):
                x_block, y_block = x_row // BLOCK, y_row // BLOCK
                listed = (asks[(x[0], y[0])] == float(y_block)) | (asks[(y[0], x[0])] == float(x_block))
                if when == "share":
                    if (x_block, y_block) == (0, 1):
                        continue
                    if x_block == y_block:
                        listed = listed & (core == x_block)
                itself = x[0] == y[0] and x_block == y_block
                if x[0] == y[0] and x_row > y_row:
                    continue

                meet(x, x_at, x_row, x_rows, y, y_at, y_row, y_rows, listed, itself)

    for x, y, when in plan:
        if when == "straight":
            pl.when(straight[x[0]] == 1)(functools.partial(visit, x, y, when))
        else:
            visit(x, y, when)

    for x, acc in row_accs.items():
        raise_row(best, x[0], PIECES[x[1]][0], jnp.max(acc[...].T, axis=0, keepdims=True))
    for y, acc in col_accs.items():
        raise_row(best, y[0], PIECES[y[1]][0], jnp.max(acc[...], axis=0, keepdims=True))
    if kind == "last":
        out[...] = jnp.full(out.shape, LOWEST, jnp.float32)
        for item in range(6):
            for part in range(8):
                out[ids[item], part : part + 1, :] = best[item : item + 1, part * 128 : (part + 1) * 128]


def score_call(plan, arrays, extra, ids, kind="middle"):
    order = sorted({b for pair in plan for b in pair[:2]} | {(b[0], 0) for pair in plan for b in pair[:2]})
    lefts = list(dict.fromkeys(x for x, _, _ in plan))
    rights = list(dict.fromkeys(y for _, y, _ in plan))
    scratch = [pltpu.VMEM((PIECES[x[1]][1], 128), jnp.float32) for x in lefts]
    scratch += [pltpu.VMEM((8, PIECES[y[1]][1]), jnp.float32) for y in rights]
    out = jax.ShapeDtypeStruct((8, ROWS), jnp.float32)
    if kind == "last":
        scratch = [pltpu.VMEM((8, ROWS), jnp.float32)] + scratch
        out = jax.ShapeDtypeStruct((2 * CHIPS, 8, 128), jnp.float32)
    return pl.pallas_call(
        functools.partial(score_kernel, plan, order, kind),
        out_shape=out,
        in_specs=[SMEM] + [VMEM] * len(order) + [SMEM if kind == "first" else VMEM],
        out_specs=VMEM,
        scratch_shapes=scratch,
        compiler_params=PARAMS,
        cost_estimate=pl.CostEstimate(flops=1, bytes_accessed=1, transcendentals=0),
    )(ids, *[in_vmem(arrays[b]) for b in order], extra)


def after(values, *others):
    return lax.optimization_barrier((values, others))[0]


def shards(embedding, row_scale, block_rows, requests):
    myself = lax.axis_index("mem").astype(jnp.int32)
    chip, core = myself // 2, myself % 2
    positions = jnp.arange(BLOCK, dtype=jnp.int32)

    def device(step, other):
        return lax.rem(chip + step + CHIPS, CHIPS) * 2 + (core ^ other)

    def by_chip(table):
        return sum(jnp.where(chip == n, table[n], 0) for n in range(CHIPS) if table[n])

    above2 = by_chip(ABOVE2_CROSSED)
    below2 = by_chip(BELOW2_CROSSED)
    ids = [myself, device(0, 1), device(-1, 0), device(1, 1), device(-2, below2), device(2, above2)]
    ids = jnp.stack(ids + [by_chip(ABOVE2_STRAIGHT), by_chip(BELOW2_STRAIGHT)]).astype(jnp.int32)

    def send(values, pairs):
        return lax.ppermute(values, "mem", pairs)

    scale = row_scale.reshape(-1, 128)
    own = decode_call(list(range(len(PIECES))), block_rows, scale, requests, embedding)
    undone = tuple(1 ^ crossed for crossed in ABOVE2_CROSSED)
    above1 = [send(piece, hop(-1, ABOVE1_CROSSED)) for piece in own]
    below1 = [send(piece, hop(1)) for piece in own]
    above2 = [send(after(piece, above1, below1), hop(-1, undone)) for piece in above1]
    below2 = [send(after(piece, above1, below1), hop(1, BELOW2_CROSSED)) for piece in below1]
    sib = [send(after(piece, above1[0], below1[0]), SIBLING) for piece in own]

    held = {OWN: own, SIB: sib, BELOW1: below1, ABOVE1: above1, BELOW2: below2, ABOVE2: above2}
    arrays = {(item, n): values for item, parts in held.items() for n, values in enumerate(parts)}
    every = range(len(PIECES))

    def pairs(left, right, when=None, lefts=every, rights=every):
        return [((left, a), (right, b), when) for a in lefts for b in rights]

    plan = pairs(OWN, OWN) + pairs(OWN, ABOVE1) + pairs(OWN, BELOW1) + pairs(ABOVE1, BELOW1)
    best = score_call(plan, arrays, block_rows, ids, "first")
    for n in every:
        plan = pairs(ABOVE2, BELOW1, lefts=[n]) + pairs(BELOW2, ABOVE1, lefts=[n])
        plan += pairs(ABOVE2, OWN, "straight", lefts=[n]) + pairs(BELOW2, OWN, "straight", lefts=[n])
        plan += pairs(BELOW2, ABOVE2, lefts=[n], rights=range(n + 1)) + pairs(ABOVE2, BELOW2, lefts=[n], rights=range(n))
        if n == 0:
            plan += pairs(OWN, SIB, "share")
        best = score_call(plan, arrays, best, ids, "last" if n == LAST else "middle")

    returned = lax.all_to_all(best, "mem", split_axis=0, concat_axis=0, tiled=True)
    highest = jnp.max(returned, axis=0).reshape(2, BLOCK)
    live = positions[None, :] < block_rows[:, None]
    return jnp.where(live, highest, jnp.float32(0.0)).reshape(-1)


def solution(mesh):
    return jax.shard_map(
        shards,
        mesh=mesh,
        in_specs=(
            P(("grp", "mem"), None),
            P(("grp", "mem")),
            P(("grp", "mem")),
            P(("grp", "mem"), None),
        ),
        out_specs=P(("grp", "mem")),
        check_vma=False,
    )
```
